128 devices in a mesh: dom: 32 (over x, y, z_hi), orb: 4 (over z_lo, core).
Axes of the slice: x: 4, y: 4, z: 4 (z_hi: 2, z_lo: 2; z = z_hi * 2 + z_lo), core: 2. Of those that a mesh axis runs over, the one named last changes fastest.
Arguments:
- block: float32 [16, 384, 32, 128], P('orb', 'dom'), may hold values from -6 to 6
- potential: float32 [384, 32, 128], P('dom'), may hold values from -1.5 to 0.5
- stored: bfloat16 [256, 384, 32, 128], P('orb', 'dom'), may hold values from -0.0048828125 to 0.0048828125
Outputs:
- filtered: float32 [16, 384, 32, 128], P('orb', 'dom')
- intersection: float32 [256, 16], P('orb')
The draws below stay inside these ranges and needn't reach their ends.
All inputs are finite; a program needn't handle non-finite values.
Results may differ from the reference program's by a relative error of at most 0.0029.
Values may be sent and summed in bfloat16 or wider, within the bound.
A program may use at most 256 MiB of HBM per device.

```python
import jax
import jax.numpy as jnp
from jax import lax

NB = 16
NS = 256
DEG = 4
CX = 12
NY = 32
NZ = 128
NX = 384


def levels(own_key, shape, shards, low, top_value):
    factor_of, own = 1.0, jax.random.fold_in(own_key, 6)
    for dim, parts in shards:
        steps = jnp.exp(jax.random.uniform(jax.random.fold_in(own, dim), (parts,), jnp.float32, low / len(shards), top_value / len(shards)))
        factor_of = factor_of * jnp.repeat(steps, shape[dim] // parts).reshape([-1 if axis == dim else 1 for axis in range(len(shape))])
    return factor_of


def noise(own_key, extent, deviation, most, cuts=(), dtype=jnp.bfloat16):
    values = deviation * jax.random.normal(own_key, extent, jnp.float32)
    if cuts:
        values = values * levels(own_key, extent, cuts, -0.22, 0.18)
    return jnp.clip(values, -most, most).astype(dtype)


def setup_inputs(seed: int = 0) -> dict:
    streams_of = jax.random.split(jax.random.key(seed), 4)
    block = noise(streams_of[0], (NB, NX, NY, NZ), 1.0, 6.0, ((0, 4), (1, 32)), jnp.float32)
    potential = jnp.clip(-1.5 + 2.0 * jax.random.uniform(streams_of[1], (NX, NY, NZ), jnp.float32) ** levels(streams_of[1], (NX, NY, NZ), ((0, 32),), -0.2, 0.2), -1.5, 0.5)
    stored = noise(streams_of[2], (NS, NX, NY, NZ), (NX * NY * NZ) ** -0.5, 0.0048828125, ((0, 4), (1, 32)))
    return {"block": block, "potential": potential, "stored": stored}


coeffs = (-5369.0 / 1800.0, 12.0 / 7.0, -15.0 / 56.0, 10.0 / 189.0, -1.0 / 112.0, 2.0 / 825.0, -1.0 / 5544.0)
inv_spacing = 6.25
center_value = 36.0
half_width = 32.0


def laplace(field):
    planes = field.shape[1]
    padded = jnp.pad(field, ((0, 0), (6, 6), (0, 0), (0, 0)))
    total = 3.0 * coeffs[0] * field
    for shift_m in range(1, 7):
        weight_m = coeffs[shift_m]
        total = total + weight_m * (padded[:, 6 + shift_m:6 + shift_m + planes] + padded[:, 6 - shift_m:6 - shift_m + planes])
        total = total + weight_m * (jnp.roll(field, shift_m, 2) + jnp.roll(field, -shift_m, 2))
        total = total + weight_m * (jnp.roll(field, shift_m, 3) + jnp.roll(field, -shift_m, 3))
    return total * inv_spacing


def hamilton(field, potential):
    return -0.5 * laplace(field) + potential[None] * field


def reference(block, potential, stored):
    previous = block
    current = (hamilton(block, potential) - center_value * block) / half_width
    for degree_step in range(DEG - 1):
        following = 2.0 * (hamilton(current, potential) - center_value * current) / half_width - previous
        previous, current = current, following
    filtered = current
    low = filtered.astype(jnp.bfloat16)

    def accumulate(index, total):
        start = (index * CX).astype(jnp.int32)
        psi_part = lax.dynamic_slice_in_dim(stored, start, CX, 1).reshape(NS, -1)
        low_part = lax.dynamic_slice_in_dim(low, start, CX, 1).reshape(NB, -1)
        return total + lax.dot_general(psi_part, low_part, (((1,), (1,)), ((), ())), preferred_element_type=jnp.float32)

    intersection = lax.fori_loop(0, NX // CX, accumulate, jnp.zeros((NS, NB), jnp.float32))
    return filtered, intersection
```

```python
import jax
import jax.numpy as jnp
import ml_dtypes
import numpy as np
from jax import lax
from jax.experimental import pallas as pl
from jax.experimental.pallas import tpu as pltpu
from jax.sharding import PartitionSpec as P

F32, BF16 = jnp.float32, jnp.bfloat16
MESH = pl.DeviceIdType.MESH

coeffs = (
    -5369.0 / 1800.0,
    12.0 / 7.0,
    -15.0 / 56.0,
    10.0 / 189.0,
    -1.0 / 112.0,
    2.0 / 825.0,
    -1.0 / 5544.0,
)
WEIGHTS = tuple(-0.5 * 6.25 * c / 16.0 for c in coeffs)
SHIFT = (-0.5 * 6.25 * 3.0 * coeffs[0] - 36.0) / 16.0
CX, NY, NZ = 12, 32, 128
PAIRS, SLABS = 16, 32


def circulant(n):
    matrix = np.zeros((n, n), np.float64)
    for m in range(1, 7):
        for i in range(n):
            matrix[i, (i + m) % n] += WEIGHTS[m]
            matrix[i, (i - m) % n] += WEIGHTS[m]
    high = matrix.astype(ml_dtypes.bfloat16)
    low = (matrix - high.astype(np.float64)).astype(ml_dtypes.bfloat16)
    return high, low


def tables():
    zh, zl = circulant(NZ)
    cz = np.block([[zh, zl], [zh, zl]])
    yh, yl = (np.kron(np.eye(4), a.astype(np.float32)).astype(ml_dtypes.bfloat16) for a in circulant(NY))
    cy = np.block([[yh, yh], [yl, yl]])
    fold = (np.arange(256)[:, None] // 16 == np.arange(128)[None, :] % 16).astype(ml_dtypes.bfloat16)
    return cz, cy, fold


def kernel(
    block, potential, stored, cz_ref, cy_ref, fold_ref, filtered, inter,
    blkf, potf, st, blkb, ownpot, rb, potb, diag, a0, a1, a2, a3, a4, sendp, low, outf, acc, part, ar1, ar2,
    local_sem, send_sem, recv_sem,
):
    dom, orb = lax.axis_index("dom"), lax.axis_index("orb")
    h = lax.rem(dom, 2)
    pair = dom // 2
    up, down = lax.rem(dom + 2, SLABS), lax.rem(dom + SLABS - 2, SLABS)
    partner = dom + 1 - 2 * h
    core = lax.rem(orb, 2)
    sibling = orb + 1 - 2 * core
    across = lax.rem(orb + 2, 4)
    row, column = lax.rem(dom, 8), dom // 8

    def rowpeer(k):
        return column * 8 + lax.rem(row + k, 8)

    def columnpeer(k):
        return lax.rem(column + k, 4) * 8 + row

    barrier = pltpu.get_barrier_semaphore()
    peers = [(rowpeer(k), orb) for k in range(1, 8)] + [(columnpeer(k), orb) for k in range(1, 4)]
    peers += [(up, orb), (down, orb), (dom, sibling), (dom, across), (partner, across)]
    for peer in peers:
        pl.semaphore_signal(barrier, inc=1, device_id=peer, device_id_type=MESH)

    loads = [
        pltpu.make_async_copy(block, blkf, local_sem.at[0]),
        pltpu.make_async_copy(potential, potf, local_sem.at[1]),
        pltpu.make_async_copy(stored, st, local_sem.at[2]),
    ]
    for load in loads:
        load.start()
    loads[0].wait()
    for i in range(4):
        blkb[i] = blkf[i].astype(BF16)
    loads[1].wait()
    ownpot[...] = potf[...].astype(BF16)

    pl.semaphore_wait(barrier, len(peers))

    count = [0]

    def remote(src, dst, peer):
        i = count[0]
        count[0] += 1
        return pltpu.make_async_remote_copy(
            src_ref=src, dst_ref=dst, send_sem=send_sem.at[i], recv_sem=recv_sem.at[i],
            device_id=peer, device_id_type=MESH,
        )

    other = 1 - h
    swap = [remote(blkb.at[2 * other + o], rb.at[o, 2 + h], (partner, orb)) for o in range(2)]
    swap_pot = remote(ownpot, potb.at[2 + h], (partner, orb))
    own = [
        (remote(blkb.at[2 * h + o], rb.at[o, h], (up, orb)), remote(blkb.at[2 * h + o], rb.at[o, 4 + h], (down, orb)))
        for o in range(2)
    ]
    forward = [
        (remote(rb.at[o, 2 + other], rb.at[o, other], (up, orb)), remote(rb.at[o, 2 + other], rb.at[o, 4 + other], (down, orb)))
        for o in range(2)
    ]

    def pot_copies(src, kind):
        near_peer = lax.select(kind == 1, up, down)
        near_slab = 4 - 3 * kind
        rest = 6 * (1 - kind)
        return (
            remote(src.at[pl.ds(6, 6)], potb.at[kind, pl.ds(6, 6)], (up, orb)),
            remote(src.at[pl.ds(0, 6)], potb.at[4 + kind, pl.ds(0, 6)], (down, orb)),
            remote(src.at[pl.ds(rest, 6)], potb.at[near_slab, pl.ds(rest, 6)], (near_peer, orb)),
        )

    own_pot = pot_copies(ownpot, h)
    forward_pot = pot_copies(potb.at[2 + other], other)

    swap_pot.start()
    for copy in swap:
        copy.start()
    for copy in own_pot + own[0]:
        copy.start()
    swap_pot.wait_recv()
    for copy in forward_pot:
        copy.start()
    swap[0].wait_recv()
    for copy in forward[0] + own[1]:
        copy.start()
    swap[1].wait_recv()
    for copy in forward[1]:
        copy.start()

    in_low = jnp.where(pair > 0, 1.0, 0.0).astype(F32)
    in_high = jnp.where(pair < PAIRS - 1, 1.0, 0.0).astype(F32)

    def inside(e):
        return jnp.where(e < 24, in_low, jnp.where(e >= 48, in_high, jnp.float32(1.0)))

    for copy in own_pot + forward_pot:
        copy.wait_recv()
    for slab, start, length in ((0, 6, 6), (1, 0, 12), (2, 0, 12), (3, 0, 12), (4, 0, 12), (5, 0, 6)):
        at = 12 * slab + start - 6
        if slab in (2, 3):
            @pl.when(h == slab - 2)
            def _(at=at):
                diag[pl.ds(at, 12)] = potf[...] * (1.0 / 16.0) + SHIFT

            @pl.when(h != slab - 2)
            def _(at=at, slab=slab):
                diag[pl.ds(at, 12)] = potb[slab].astype(F32) * (1.0 / 16.0) + SHIFT
        else:
            diag[pl.ds(at, length)] = potb[slab, pl.ds(start, length)].astype(F32) * (1.0 / 16.0) + SHIFT

    def step(src, src_at, prev, prev_at, dst, dst_at, groups):
        def group(g, carry):
            e = dst_at + 12 * g
            s = e - src_at
            pieces = []
            for q in range(3):
                v = src[pl.ds(s + 4 * q, 4)].reshape(128, 128)
                high = v.astype(BF16)
                rest = (v - high.astype(F32)).astype(BF16)
                rz = jnp.dot(jnp.concatenate([high, rest], 1), cz_ref[...], preferred_element_type=F32)
                ry = jnp.dot(cy_ref[...], jnp.concatenate([high, rest], 0), preferred_element_type=F32)
                pieces.append((rz[:, :128] + rz[:, 128:]) + (ry[:128] + ry[128:]))
            for i in range(12):
                t = pieces[i // 4][32 * (i % 4) : 32 * (i % 4) + 32]
                t = t + src[s + i] * diag[e + i - 6]
                for m in range(1, 7):
                    t = t + WEIGHTS[m] * (src[s + i + m] + src[s + i - m])
                if prev is None:
                    t = t * (0.5 * inside(e + i))
                else:
                    t = (t - prev[e + i - prev_at]) * inside(e + i)
                dst[e + i - dst_at] = t
            return carry

        lax.fori_loop(0, groups, group, 0)

    group_low = 4 * orb + 2 * h
    gather, relay = [], []
    for o in range(2):
        mine = low.at[group_low + o]
        gather.append((
            remote(sendp.at[o], low.at[group_low + o], (partner, orb)),
            remote(sendp.at[o], low.at[group_low + o], (partner, across)),
            remote(mine, low.at[group_low + o], (dom, across)),
            remote(mine, low.at[group_low + o], (dom, sibling)),
        ))
        arrived = (4 * orb + 2 * other + o, 4 * across + 2 * other + o, 4 * across + 2 * h + o)
        relay.append(tuple(remote(low.at[i], low.at[i], (dom, sibling)) for i in arrived))

    outs = []
    for o in range(2):
        for copy in own[o] + forward[o]:
            copy.wait_recv()
        for slab in range(6):
            edge = in_low if slab < 2 else in_high if slab > 3 else None
            if edge is None:
                @pl.when(h == slab - 2)
                def _(slab=slab, o=o):
                    a0[pl.ds(12 * slab, 12)] = blkf[2 * h + o]

                @pl.when(h != slab - 2)
                def _(slab=slab, o=o):
                    a0[pl.ds(12 * slab, 12)] = rb[o, slab].astype(F32)
            else:
                a0[pl.ds(12 * slab, 12)] = rb[o, slab].astype(F32) * edge
        step(a0, 0, None, 0, a1, 6, 5)
        step(a1, 6, a0, 0, a2, 12, 4)
        step(a2, 12, a1, 6, a3, 18, 3)
        step(a3, 18, a2, 12, a4.at[o], 24, 2)
        sendp[o] = a4[o, pl.ds(12 * other, 12)].astype(BF16)
        gather[o][0].start()
        gather[o][1].start()
        low[group_low + o] = a4[o, pl.ds(12 * h, 12)].astype(BF16)
        gather[o][2].start()
        gather[o][3].start()
        out = pltpu.make_async_copy(a4.at[o, pl.ds(12 * h, 12)], filtered.at[2 * h + o], local_sem.at[3 + o])
        out.start()
        outs.append(out)

    for o in range(2):
        for i in (2, 1, 0):
            gather[o][i].wait_recv()
            relay[o][i].start()
        outf[o] = low[4 * orb + 2 * other + o].astype(F32)
        out = pltpu.make_async_copy(outf.at[o], filtered.at[2 * other + o], local_sem.at[5 + o])
        out.start()
        outs.append(out)
    for o in range(2):
        gather[o][3].wait_recv()
        for copy in relay[o]:
            copy.wait_recv()

    loads[2].wait()

    def contract(q, carry):
        total = None
        for g in range(2):
            left = [st[:, 2 * q + i, 16 * g : 16 * g + 16].reshape(1024, 128) for i in range(2)]
            right = [low[:, 2 * q + i, 16 * g : 16 * g + 16].reshape(256, 128) for i in range(2)]
            term = lax.dot_general(
                jnp.concatenate(left, 1), jnp.concatenate(right, 1), (((1,), (1,)), ((), ())), preferred_element_type=F32
            )
            total = term if total is None else total + term
        acc[...] = acc[...] + total
        return carry

    acc[...] = jnp.zeros_like(acc)
    lax.fori_loop(0, 6, contract, 0)
    same = lax.broadcasted_iota(jnp.int32, (16, 256), 0) == lax.rem(lax.broadcasted_iota(jnp.int32, (16, 256), 1), 16)
    rows = jnp.sum(jnp.where(same[None], acc[...].reshape(64, 16, 256), 0.0), axis=1)
    first = rows.astype(BF16)
    rest = rows - first.astype(F32)
    second = rest.astype(BF16)
    third = (rest - second.astype(F32)).astype(BF16)
    folded = jnp.dot(jnp.concatenate([first, second, third], 0), fold_ref[...], preferred_element_type=F32)
    folded = (folded[128:192] + folded[64:128]) + folded[:64]
    lane = lax.broadcasted_iota(jnp.int32, (8, 128), 1) // 16
    total = jnp.zeros((8, 128), F32)
    for b in range(8):
        total = jnp.where(lane == b, folded[8 * b : 8 * b + 8], total)

    for buffer, size, me, peer in ((ar1, 8, row, rowpeer), (ar2, 4, column, columnpeer)):
        part_at = part.at[0 if size == 8 else 1]
        part_at[...] = total
        buffer[me] = total
        copies = [remote(part_at, buffer.at[me], (peer(k), orb)) for k in range(1, size)]
        for copy in copies:
            copy.start()
        for copy in copies:
            copy.wait_recv()
        total = buffer[0]
        for k in range(1, size):
            total = total + buffer[k]
        for copy in copies:
            copy.wait_send()
    for b in range(8):
        inter[8 * b : 8 * b + 8, :] = total[:, 16 * b : 16 * b + 16]

    for copy in [swap_pot] + swap + list(own_pot + forward_pot):
        copy.wait_send()
    for o in range(2):
        for copy in own[o] + forward[o] + gather[o] + relay[o]:
            copy.wait_send()
    for out in outs:
        out.wait()
    assert count[0] == 41, count[0]


def body(block, potential, stored):
    cz, cy, fold = (jnp.asarray(t) for t in tables())
    planes = (CX, NY, NZ)
    vmem, anywhere = pl.BlockSpec(memory_space=pltpu.VMEM), pl.BlockSpec(memory_space=pl.ANY)
    return pl.pallas_call(
        kernel,
        out_shape=(jax.ShapeDtypeStruct((4,) + planes, F32), jax.ShapeDtypeStruct((64, 16), F32)),
        in_specs=[anywhere] * 3 + [vmem] * 3,
        out_specs=(anywhere, vmem),
        scratch_shapes=[
            pltpu.VMEM((4,) + planes, F32),
            pltpu.VMEM(planes, F32),
            pltpu.VMEM((64,) + planes, BF16),
            pltpu.VMEM((4,) + planes, BF16),
            pltpu.VMEM(planes, BF16),
            pltpu.VMEM((2, 6) + planes, BF16),
            pltpu.VMEM((6,) + planes, BF16),
            pltpu.VMEM((60, NY, NZ), F32),
            pltpu.VMEM((72, NY, NZ), F32),
            pltpu.VMEM((60, NY, NZ), F32),
            pltpu.VMEM((48, NY, NZ), F32),
            pltpu.VMEM((36, NY, NZ), F32),
            pltpu.VMEM((2, 24, NY, NZ), F32),
            pltpu.VMEM((2,) + planes, BF16),
            pltpu.VMEM((16,) + planes, BF16),
            pltpu.VMEM((2,) + planes, F32),
            pltpu.VMEM((1024, 256), F32),
            pltpu.VMEM((2, 8, 128), F32),
            pltpu.VMEM((8, 8, 128), F32),
            pltpu.VMEM((4, 8, 128), F32),
            pltpu.SemaphoreType.DMA((7,)),
            pltpu.SemaphoreType.DMA((41,)),
            pltpu.SemaphoreType.DMA((41,)),
        ],
        compiler_params=pltpu.CompilerParams(collective_id=0, has_side_effects=True, vmem_limit_bytes=48 * 2**20),
    )(block, potential, stored, cz, cy, fold)


def solution(mesh):
    in_specs = (P("orb", "dom", None, None), P("dom", None, None), P("orb", "dom", None, None))
    out_specs = (P("orb", "dom", None, None), P("orb", None))
    return jax.shard_map(body, mesh=mesh, in_specs=in_specs, out_specs=out_specs, check_vma=False)
```

```python
import jax
import jax.numpy as jnp
import ml_dtypes
import numpy as np
from jax import lax
from jax.experimental import pallas as pl
from jax.experimental.pallas import tpu as pltpu
from jax.sharding import PartitionSpec as P

F32, BF16 = jnp.float32, jnp.bfloat16
MESH = pl.DeviceIdType.MESH

coeffs = (
    -5369.0 / 1800.0,
    12.0 / 7.0,
    -15.0 / 56.0,
    10.0 / 189.0,
    -1.0 / 112.0,
    2.0 / 825.0,
    -1.0 / 5544.0,
)
WEIGHTS = tuple(-0.5 * 6.25 * c / 16.0 for c in coeffs)
SHIFT = (-0.5 * 6.25 * 3.0 * coeffs[0] - 36.0) / 16.0
CX, NY, NZ = 12, 32, 128
PAIRS, SLABS = 16, 32


HIGHS = tuple(float(np.float32(w).astype(ml_dtypes.bfloat16)) for w in WEIGHTS)
LOWS = tuple(w - high for w, high in zip(WEIGHTS, HIGHS))


def iotas(shape):
    return lax.broadcasted_iota(jnp.int32, shape, 0), lax.broadcasted_iota(jnp.int32, shape, 1)


def circulant(n, values):
    i, j = iotas((n, n))
    distance = (i - j) & (n - 1)
    matrix = jnp.zeros((n, n), F32)
    for m in range(1, 7):
        matrix = jnp.where((distance == m) | (distance == n - m), values[m], matrix)
    return matrix


def kernel(
    block, potential, stored, filtered, inter,
    cz_ref, cy_ref, blkf, potf, st, blkb, rb, potb, diag, a0, a1, a2, a3, a4, sendp, low, outf, acc, part, ar1, ar2,
    local_sem, send_sem, recv_sem,
):
    dom, orb = lax.axis_index("dom"), lax.axis_index("orb")
    h = lax.rem(dom, 2)
    pair = dom // 2
    up, down = lax.rem(dom + 2, SLABS), lax.rem(dom + SLABS - 2, SLABS)
    partner = dom + 1 - 2 * h
    core = lax.rem(orb, 2)
    sibling = orb + 1 - 2 * core
    across = lax.rem(orb + 2, 4)
    row, column = lax.rem(dom, 8), dom // 8

    def rowpeer(k):
        return column * 8 + lax.rem(row + k, 8)

    def columnpeer(k):
        return lax.rem(column + k, 4) * 8 + row

    barrier = pltpu.get_barrier_semaphore()
    peers = [(partner, orb), (up, orb), (down, orb), (dom, sibling), (dom, across), (partner, across)]
    peers += [(rowpeer(k), orb) for k in range(1, 8)] + [(columnpeer(k), orb) for k in range(1, 4)]
    for peer in peers:
        pl.semaphore_signal(barrier, inc=1, device_id=peer, device_id_type=MESH)

    other = 1 - h
    order = (2 * other, 2 * other + 1, 2 * h, 2 * h + 1)
    loads = [pltpu.make_async_copy(block.at[i], blkf.at[i], local_sem.at[n]) for n, i in enumerate(order)]
    loads.insert(2, pltpu.make_async_copy(potential, potf, local_sem.at[4]))
    load_stored = pltpu.make_async_copy(stored, st, local_sem.at[5])
    for load in loads:
        load.start()
    high, rest = circulant(NZ, HIGHS), circulant(NZ, LOWS)
    cz_ref[...] = jnp.concatenate([jnp.concatenate([high, rest], 1)] * 2, 0).astype(BF16)
    high, rest = circulant(NY, HIGHS), circulant(NY, LOWS)
    cy_ref[...] = jnp.concatenate([jnp.concatenate([high, high], 1), jnp.concatenate([rest, rest], 1)], 0).astype(BF16)
    for load in loads:
        load.wait()
    load_stored.start()
    for i in range(4):
        blkb[i] = blkf[i].astype(BF16)
    for r in range(2):
        potb[r, pl.ds(24 + 12 * h, 12)] = potf[:, 16 * r : 16 * r + 16].astype(BF16)

    pl.semaphore_wait(barrier, len(peers))

    def remote(i, src, dst, peer):
        return pltpu.make_async_remote_copy(
            src_ref=src, dst_ref=dst, send_sem=send_sem.at[i], recv_sem=recv_sem.at[i],
            device_id=peer, device_id_type=MESH,
        )

    def swap(o):
        return (remote(o, blkb.at[2 * other + o], rb.at[o, 2 + h], (partner, orb)),)

    def own(o):
        src = blkb.at[2 * h + o]
        return remote(2 + o, src, rb.at[o, h], (up, orb)), remote(4 + o, src, rb.at[o, 4 + h], (down, orb))

    def forward(o):
        src = rb.at[o, 2 + other]
        return remote(6 + o, src, rb.at[o, other], (up, orb)), remote(8 + o, src, rb.at[o, 4 + other], (down, orb))

    group_low = 4 * orb + 2 * h

    def gather(o):
        here = low.at[group_low + o]
        return (
            remote(10 + o, sendp.at[o], here, (partner, orb)),
            remote(12 + o, sendp.at[o], here, (partner, across)),
            remote(14 + o, here, here, (dom, across)),
            remote(16 + o, here, here, (dom, sibling)),
        )

    def relay(o):
        arrived = (4 * orb + 2 * other + o, 4 * across + 2 * other + o, 4 * across + 2 * h + o)
        return tuple(remote(18 + 2 * n + o, low.at[i], low.at[i], (dom, sibling)) for n, i in enumerate(arrived))

    def pot_copy(i, src, dst, length, peer):
        return remote(i, potb.at[core, pl.ds(src, length)], potb.at[core, pl.ds(dst, length)], peer)

    def pot_copies(i, kind):
        src = 24 + 12 * kind
        rest = 6 * (1 - kind)
        return (
            pot_copy(i, src + 6, 12 * kind + 6, 6, (up, orb)),
            pot_copy(i + 1, src, 48 + 12 * kind, 6, (down, orb)),
            pot_copy(i + 2, src + rest, 48 - 36 * kind + rest, 6, (lax.select(kind == 1, up, down), orb)),
        )

    swap_pot = (pot_copy(24, 24 + 12 * h, 24 + 12 * h, 12, (partner, orb)),)
    own_pot, forward_pot = pot_copies(25, h), pot_copies(28, other)
    share_pot = tuple(
        pot_copy(31 + n, at, at, length, (dom, sibling))
        for n, (at, length) in enumerate(((6, 18), (24 + 12 * other, 12), (48, 18)))
    )

    def start(copies):
        for copy in copies:
            copy.start()

    def received(copies):
        for copy in copies:
            copy.wait_recv()

    def sent(copies):
        for copy in copies:
            copy.wait_send()

    start(swap(0) + own(0) + swap_pot + own_pot + swap(1) + own(1))
    received(swap(0))
    start(forward(0))
    received(swap_pot)
    start(forward_pot)
    received(swap(1))
    start(forward(1))

    in_low = jnp.where(pair > 0, 1.0, 0.0).astype(F32)
    in_high = jnp.where(pair < PAIRS - 1, 1.0, 0.0).astype(F32)

    received(own_pot + forward_pot)
    start(share_pot)
    received(share_pot)
    for r in range(2):
        diag[:, 16 * r : 16 * r + 16] = potb[r, 6:66].astype(F32) * (1.0 / 16.0) + SHIFT
    diag[pl.ds(18 + 12 * h, 12)] = potf[...] * (1.0 / 16.0) + SHIFT

    def step(src, src_at, prev, prev_at, dst, dst_at, groups):
        for e in range(dst_at, dst_at + 12 * groups, 12):
            s = e - src_at
            v = src[s : s + 12].reshape(12 * NY, NZ)
            high = v.astype(BF16)
            rest = (v - high.astype(F32)).astype(BF16)
            along_z = jnp.dot(jnp.concatenate([high, rest], 1), cz_ref[...], preferred_element_type=F32)
            along_z = along_z[:, :NZ] + along_z[:, NZ:]
            along_y = []
            for i in range(0, 12, 2):
                parts = [
                    jnp.concatenate([a[NY * k : NY * k + NY] for a in (high, rest)], 0) for k in (i, i + 1)
                ]
                product = jnp.dot(cy_ref[...], jnp.concatenate(parts, 1), preferred_element_type=F32)
                product = product[:NY] + product[NY:]
                along_y += [product[:, :NZ], product[:, NZ:]]
            for y in range(0, NY, 8):
                window = [src[s - 6 + k, y : y + 8] for k in range(24)]
                for i in range(12):
                    t = window[6 + i] * diag[e + i - 6, y : y + 8]
                    t = t + (along_z[NY * i + y : NY * i + y + 8] + along_y[i][y : y + 8])
                    for m in range(1, 7):
                        t = t + WEIGHTS[m] * (window[6 + i + m] + window[6 + i - m])
                    if prev is None:
                        t = t * 0.5
                    else:
                        t = t - prev[e + i - prev_at, y : y + 8]
                    if e + i < 24:
                        t = t * in_low
                    elif e + i >= 48:
                        t = t * in_high
                    dst[e + i - dst_at, y : y + 8] = t

    def out_own(o):
        return pltpu.make_async_copy(a4.at[o, pl.ds(12 * h, 12)], filtered.at[2 * h + o], local_sem.at[6 + o])

    def out_other(o):
        return pltpu.make_async_copy(outf.at[o], filtered.at[2 * other + o], local_sem.at[8 + o])

    def orbital(o, carry):
        received(own(o) + forward(o))
        for slab in (0, 1, 4, 5):
            a0[12 * slab : 12 * slab + 12] = rb[o, slab].astype(F32) * (in_low if slab < 2 else in_high)
        a0[pl.ds(24 + 12 * other, 12)] = rb[o, 2 + other].astype(F32)
        a0[pl.ds(24 + 12 * h, 12)] = blkf[2 * h + o]
        step(a0, 0, None, 0, a1, 6, 5)
        step(a1, 6, a0, 0, a2, 12, 4)
        step(a2, 12, a1, 6, a3, 18, 3)
        step(a3, 18, a2, 12, a4.at[o], 24, 2)
        sendp[o] = a4[o, pl.ds(12 * other, 12)].astype(BF16)
        start(gather(o)[:2])
        low[group_low + o] = a4[o, pl.ds(12 * h, 12)].astype(BF16)
        start(gather(o)[2:])
        out_own(o).start()
        return carry

    lax.fori_loop(0, 2, orbital, 0)

    for o in range(2):
        for i in (2, 1, 0):
            received(gather(o)[i : i + 1])
            start(relay(o)[i : i + 1])
        outf[o] = low[4 * orb + 2 * other + o].astype(F32)
        out_other(o).start()
    for o in range(2):
        received(gather(o)[3:] + relay(o))

    load_stored.wait()
    total = None
    for p in range(0, 12, 2):
        for y in range(0, NY, 16):
            left = [st[:, p + i, y : y + 16].reshape(1024, NZ) for i in range(2)]
            right = [low[:, p + i, y : y + 16].reshape(256, NZ) for i in range(2)]
            term = lax.dot_general(
                jnp.concatenate(left, 1), jnp.concatenate(right, 1), (((1,), (1,)), ((), ())), preferred_element_type=F32
            )
            total = term if total is None else total + term
    acc[...] = total
    i, j = iotas((16, 256))
    same = i == j % 16
    rows = jnp.sum(jnp.where(same[None], acc[...].reshape(64, 16, 256), 0.0), axis=1)
    first = rows.astype(BF16)
    rest = rows - first.astype(F32)
    second = rest.astype(BF16)
    third = (rest - second.astype(F32)).astype(BF16)
    i, j = iotas((16, 256))
    fold = jnp.where(i == j // 16, 1.0, 0.0).astype(BF16)
    total = jnp.zeros((16, 64), F32)
    for piece in (third, second, first):
        total = total + lax.dot_general(fold, piece, (((1,), (1,)), ((), ())), preferred_element_type=F32)

    for buffer, size, me, peer in ((ar1, 8, row, rowpeer), (ar2, 4, column, columnpeer)):
        part_at = part.at[0 if size == 8 else 1]
        part_at[...] = total
        buffer[me] = total
        at = 33 if size == 8 else 40
        copies = [remote(at + k, part_at, buffer.at[me], (peer(k), orb)) for k in range(1, size)]
        start(copies)
        received(copies)
        total = buffer[0]
        for k in range(1, size):
            total = total + buffer[k]
        sent(copies)
    inter[...] = total

    sent(swap_pot + own_pot + forward_pot + share_pot)
    for o in range(2):
        sent(swap(o) + own(o) + forward(o) + gather(o) + relay(o))
        out_own(o).wait()
        out_other(o).wait()


def body(block, potential, stored):
    planes = (CX, NY, NZ)
    vmem, anywhere = pl.BlockSpec(memory_space=pltpu.VMEM), pl.BlockSpec(memory_space=pl.ANY)
    filtered, inter = pl.pallas_call(
        kernel,
        out_shape=(jax.ShapeDtypeStruct((4,) + planes, F32), jax.ShapeDtypeStruct((16, 64), F32)),
        in_specs=[anywhere] * 3,
        out_specs=(anywhere, vmem),
        scratch_shapes=[
            pltpu.VMEM((256, 256), BF16),
            pltpu.VMEM((64, 64), BF16),
            pltpu.VMEM((4,) + planes, F32),
            pltpu.VMEM(planes, F32),
            pltpu.VMEM((64,) + planes, BF16),
            pltpu.VMEM((4,) + planes, BF16),
            pltpu.VMEM((2, 6) + planes, BF16),
            pltpu.VMEM((2, 72, 16, NZ), BF16),
            pltpu.VMEM((60, NY, NZ), F32),
            pltpu.VMEM((72, NY, NZ), F32),
            pltpu.VMEM((60, NY, NZ), F32),
            pltpu.VMEM((48, NY, NZ), F32),
            pltpu.VMEM((36, NY, NZ), F32),
            pltpu.VMEM((2, 24, NY, NZ), F32),
            pltpu.VMEM((2,) + planes, BF16),
            pltpu.VMEM((16,) + planes, BF16),
            pltpu.VMEM((2,) + planes, F32),
            pltpu.VMEM((1024, 256), F32),
            pltpu.VMEM((2, 16, 64), F32),
            pltpu.VMEM((8, 16, 64), F32),
            pltpu.VMEM((4, 16, 64), F32),
            pltpu.SemaphoreType.DMA((10,)),
            pltpu.SemaphoreType.DMA((44,)),
            pltpu.SemaphoreType.DMA((44,)),
        ],
        compiler_params=pltpu.CompilerParams(collective_id=0, has_side_effects=True, vmem_limit_bytes=60 * 2**20),
    )(block, potential, stored)
    return filtered, inter.T


def solution(mesh):
    in_specs = (P("orb", "dom", None, None), P("dom", None, None), P("orb", "dom", None, None))
    out_specs = (P("orb", "dom", None, None), P("orb", None))
    return jax.shard_map(body, mesh=mesh, in_specs=in_specs, out_specs=out_specs, check_vma=False)
```

```python
import jax
import jax.numpy as jnp
import ml_dtypes
import numpy as np
from jax import lax
from jax.experimental import pallas as pl
from jax.experimental.pallas import tpu as pltpu
from jax.sharding import PartitionSpec as P

F32, BF16 = jnp.float32, jnp.bfloat16
MESH = pl.DeviceIdType.MESH

coeffs = (
    -5369.0 / 1800.0,
    12.0 / 7.0,
    -15.0 / 56.0,
    10.0 / 189.0,
    -1.0 / 112.0,
    2.0 / 825.0,
    -1.0 / 5544.0,
)
WEIGHTS = tuple(-0.5 * 6.25 * c / 16.0 for c in coeffs)
SHIFT = (-0.5 * 6.25 * 3.0 * coeffs[0] - 36.0) / 16.0
CX, NY, NZ = 12, 32, 128
PAIRS, SLABS = 16, 32


HIGHS = tuple(float(np.float32(w).astype(ml_dtypes.bfloat16)) for w in WEIGHTS)
LOWS = tuple(w - high for w, high in zip(WEIGHTS, HIGHS))


def iotas(shape):
    return lax.broadcasted_iota(jnp.int32, shape, 0), lax.broadcasted_iota(jnp.int32, shape, 1)


def circulant(n, values):
    i, j = iotas((n, n))
    distance = (i - j) & (n - 1)
    matrix = jnp.zeros((n, n), F32)
    for m in range(1, 7):
        matrix = jnp.where((distance == m) | (distance == n - m), values[m], matrix)
    return matrix


def kernel(
    block, potential, stored, filtered, inter,
    cz_ref, cy_ref, blkf, potf, st, blkb, rb, potb, diag, a0, a1, a2, a3, a4, sendp, low, outf, acc, part, ar1, ar2,
    local_sem, send_sem, recv_sem,
):
    dom, orb = lax.axis_index("dom"), lax.axis_index("orb")
    h = lax.rem(dom, 2)
    pair = dom // 2
    up, down = lax.rem(dom + 2, SLABS), lax.rem(dom + SLABS - 2, SLABS)
    partner = dom + 1 - 2 * h
    core = lax.rem(orb, 2)
    sibling = orb + 1 - 2 * core
    across = lax.rem(orb + 2, 4)
    row, column = lax.rem(dom, 8), dom // 8

    def rowpeer(k):
        return column * 8 + lax.rem(row + k, 8)

    def columnpeer(k):
        return lax.rem(column + k, 4) * 8 + row

    barrier = pltpu.get_barrier_semaphore()
    peers = [(rowpeer(k), orb) for k in (1, 7)] + [(up, orb), (down, orb), (dom, sibling), (dom, across), (partner, across)]
    peers += [(rowpeer(k), orb) for k in range(2, 7)] + [(columnpeer(k), orb) for k in range(1, 4)]
    for peer in peers:
        pl.semaphore_signal(barrier, inc=1, device_id=peer, device_id_type=MESH)

    other = 1 - h
    order = (2 * other, 2 * other + 1, 2 * h, 2 * h + 1)
    loads = [pltpu.make_async_copy(block.at[i], blkf.at[i], local_sem.at[n]) for n, i in enumerate(order)]
    loads.insert(2, pltpu.make_async_copy(potential, potf, local_sem.at[4]))
    load_stored = pltpu.make_async_copy(stored, st, local_sem.at[5])
    for load in loads:
        load.start()
    high, rest = circulant(NZ, HIGHS), circulant(NZ, LOWS)
    cz_ref[...] = jnp.concatenate([jnp.concatenate([high, rest], 1)] * 2, 0).astype(BF16)
    high, rest = circulant(NY, HIGHS), circulant(NY, LOWS)
    cy_ref[...] = jnp.concatenate([jnp.concatenate([high, high], 1), jnp.concatenate([rest, rest], 1)], 0).astype(BF16)
    for load in loads:
        load.wait()
    load_stored.start()
    for i in range(4):
        blkb[i] = blkf[i].astype(BF16)
    for r in range(2):
        potb[r, pl.ds(24 + 12 * h, 12)] = potf[:, 16 * r : 16 * r + 16].astype(BF16)

    pl.semaphore_wait(barrier, len(peers))

    def remote(i, src, dst, peer):
        return pltpu.make_async_remote_copy(
            src_ref=src, dst_ref=dst, send_sem=send_sem.at[i], recv_sem=recv_sem.at[i],
            device_id=peer, device_id_type=MESH,
        )

    def swap(o):
        return (remote(o, blkb.at[2 * other + o], rb.at[o, 2 + h], (partner, orb)),)

    def own(o):
        src = blkb.at[2 * h + o]
        return remote(2 + o, src, rb.at[o, h], (up, orb)), remote(4 + o, src, rb.at[o, 4 + h], (down, orb))

    def forward(o):
        src = rb.at[o, 2 + other]
        return remote(6 + o, src, rb.at[o, other], (up, orb)), remote(8 + o, src, rb.at[o, 4 + other], (down, orb))

    group_low = 4 * orb + 2 * h

    def gather(o):
        here = low.at[group_low + o]
        return (
            remote(10 + o, sendp.at[o], here, (partner, orb)),
            remote(12 + o, sendp.at[o], here, (partner, across)),
            remote(14 + o, here, here, (dom, across)),
            remote(16 + o, here, here, (dom, sibling)),
        )

    def relay(o):
        arrived = (4 * orb + 2 * other + o, 4 * across + 2 * other + o, 4 * across + 2 * h + o)
        return tuple(remote(18 + 2 * n + o, low.at[i], low.at[i], (dom, sibling)) for n, i in enumerate(arrived))

    def pot_copy(i, src, dst, length, peer):
        return remote(i, potb.at[core, pl.ds(src, length)], potb.at[core, pl.ds(dst, length)], peer)

    def pot_copies(i, kind):
        src = 24 + 12 * kind
        rest = 6 * (1 - kind)
        return (
            pot_copy(i, src + 6, 12 * kind + 6, 6, (up, orb)),
            pot_copy(i + 1, src, 48 + 12 * kind, 6, (down, orb)),
            pot_copy(i + 2, src + rest, 48 - 36 * kind + rest, 6, (lax.select(kind == 1, up, down), orb)),
        )

    swap_pot = (pot_copy(24, 24 + 12 * h, 24 + 12 * h, 12, (partner, orb)),)
    own_pot, forward_pot = pot_copies(25, h), pot_copies(28, other)
    share_pot = tuple(
        pot_copy(31 + n, at, at, length, (dom, sibling))
        for n, (at, length) in enumerate(((6, 18), (24 + 12 * other, 12), (48, 18)))
    )

    def start(copies):
        for copy in copies:
            copy.start()

    def received(copies):
        for copy in copies:
            copy.wait_recv()

    def sent(copies):
        for copy in copies:
            copy.wait_send()

    start(swap_pot + own_pot + swap(0) + own(0))
    received(swap_pot)
    start(forward_pot + swap(1))
    received(swap(0))
    start(forward(0) + own(1))
    received(swap(1))
    start(forward(1))

    in_low = jnp.where(pair > 0, 1.0, 0.0).astype(F32)
    in_high = jnp.where(pair < PAIRS - 1, 1.0, 0.0).astype(F32)

    received(own_pot + forward_pot)
    start(share_pot)
    received(share_pot)
    for r in range(2):
        diag[:, 16 * r : 16 * r + 16] = potb[r, 6:66].astype(F32) * (1.0 / 16.0) + SHIFT
    diag[pl.ds(18 + 12 * h, 12)] = potf[...] * (1.0 / 16.0) + SHIFT

    def step(src, src_at, prev, prev_at, dst, dst_at, starts, masked=True):
        for e in starts:
            s = e - src_at
            for i in range(0, 12, 2):
                v = src[pl.ds(s + i, 2)].reshape(2 * NY, NZ)
                high = v.astype(BF16)
                rest = (v - high.astype(F32)).astype(BF16)
                along_z = jnp.dot(jnp.concatenate([high, rest], 1), cz_ref[...], preferred_element_type=F32)
                along_z = along_z[:, :NZ] + along_z[:, NZ:]
                parts = [jnp.concatenate([a[NY * k : NY * k + NY] for a in (high, rest)], 0) for k in range(2)]
                along_y = jnp.dot(cy_ref[...], jnp.concatenate(parts, 1), preferred_element_type=F32)
                along_y = along_y[:NY] + along_y[NY:]
                for k in range(2):
                    dst[e + i + k - dst_at] = along_z[NY * k : NY * k + NY] + along_y[:, NZ * k : NZ * k + NZ]
            for y in range(0, NY, 8):
                window = [src[s - 6 + k, y : y + 8] for k in range(24)]
                for i in range(12):
                    t = window[6 + i] * diag[e + i - 6, y : y + 8]
                    for m in range(1, 7):
                        t = t + WEIGHTS[m] * (window[6 + i + m] + window[6 + i - m])
                    t = t + dst[e + i - dst_at, y : y + 8]
                    if prev is None:
                        t = t * 0.5
                    else:
                        t = t - prev[e + i - prev_at, y : y + 8]
                    if masked and e + i < 24:
                        t = t * in_low
                    elif masked and e + i >= 48:
                        t = t * in_high
                    dst[e + i - dst_at, y : y + 8] = t

    def out_own(o):
        return pltpu.make_async_copy(a4.at[o, pl.ds(12 * h, 12)], filtered.at[2 * h + o], local_sem.at[6 + o])

    def out_other(o):
        return pltpu.make_async_copy(outf.at[o], filtered.at[2 * other + o], local_sem.at[8 + o])

    def orbital(o, carry):
        received(own(o) + forward(o))
        for slab in (0, 1, 4, 5):
            a0[12 * slab : 12 * slab + 12] = rb[o, slab].astype(F32) * (in_low if slab < 2 else in_high)
        a0[pl.ds(24 + 12 * other, 12)] = rb[o, 2 + other].astype(F32)
        a0[pl.ds(24 + 12 * h, 12)] = blkf[2 * h + o]
        step(a0, 0, None, 0, a1, 6, range(6, 66, 12))
        step(a1, 6, a0, 0, a2, 12, range(12, 60, 12))
        step(a2, 12, a1, 6, a3, 18, range(18, 54, 12))
        step(a3, 18, a2, 12, a4.at[o], 24, (24 + 12 * other,), masked=False)
        sendp[o] = a4[o, pl.ds(12 * other, 12)].astype(BF16)
        start(gather(o)[:2])
        step(a3, 18, a2, 12, a4.at[o], 24, (24 + 12 * h,), masked=False)
        low[group_low + o] = a4[o, pl.ds(12 * h, 12)].astype(BF16)
        start(gather(o)[2:])
        out_own(o).start()
        return carry

    lax.fori_loop(0, 2, orbital, 0)

    for o in range(2):
        for i in (2, 1, 0):
            received(gather(o)[i : i + 1])
            start(relay(o)[i : i + 1])
        outf[o] = low[4 * orb + 2 * other + o].astype(F32)
        out_other(o).start()
    for o in range(2):
        received(gather(o)[3:] + relay(o))

    load_stored.wait()
    total = None
    for p in range(0, 12, 2):
        for y in range(0, NY, 16):
            left = [st[:, p + i, y : y + 16].reshape(1024, NZ) for i in range(2)]
            right = [low[:, p + i, y : y + 16].reshape(256, NZ) for i in range(2)]
            term = lax.dot_general(
                jnp.concatenate(left, 1), jnp.concatenate(right, 1), (((1,), (1,)), ((), ())), preferred_element_type=F32
            )
            total = term if total is None else total + term
    acc[...] = total
    i, j = iotas((16, 256))
    same = i == j % 16
    rows = jnp.sum(jnp.where(same[None], acc[...].reshape(64, 16, 256), 0.0), axis=1)
    first = rows.astype(BF16)
    rest = rows - first.astype(F32)
    second = rest.astype(BF16)
    third = (rest - second.astype(F32)).astype(BF16)
    i, j = iotas((16, 256))
    fold = jnp.where(i == j // 16, 1.0, 0.0).astype(BF16)
    total = jnp.zeros((16, 64), F32)
    for piece in (third, second, first):
        total = total + lax.dot_general(fold, piece, (((1,), (1,)), ((), ())), preferred_element_type=F32)

    sums = []
    for buffer, size, me, peer in ((ar1, 8, row, rowpeer), (ar2, 4, column, columnpeer)):
        part_at = part.at[0 if size == 8 else 1]
        part_at[...] = total
        buffer[me] = total
        at = 33 if size == 8 else 40
        copies = [remote(at + k, part_at, buffer.at[me], (peer(k), orb)) for k in range(1, size)]
        start(copies)
        received(copies)
        total = buffer[0]
        for k in range(1, size):
            total = total + buffer[k]
        sums += copies
    inter[...] = total

    sent(sums)
    sent(swap_pot + own_pot + forward_pot + share_pot)
    for o in range(2):
        sent(swap(o) + own(o) + forward(o) + gather(o) + relay(o))
        out_own(o).wait()
        out_other(o).wait()


def body(block, potential, stored):
    planes = (CX, NY, NZ)
    vmem, anywhere = pl.BlockSpec(memory_space=pltpu.VMEM), pl.BlockSpec(memory_space=pl.ANY)
    filtered, inter = pl.pallas_call(
        kernel,
        out_shape=(jax.ShapeDtypeStruct((4,) + planes, F32), jax.ShapeDtypeStruct((16, 64), F32)),
        in_specs=[anywhere] * 3,
        out_specs=(anywhere, vmem),
        scratch_shapes=[
            pltpu.VMEM((256, 256), BF16),
            pltpu.VMEM((64, 64), BF16),
            pltpu.VMEM((4,) + planes, F32),
            pltpu.VMEM(planes, F32),
            pltpu.VMEM((64,) + planes, BF16),
            pltpu.VMEM((4,) + planes, BF16),
            pltpu.VMEM((2, 6) + planes, BF16),
            pltpu.VMEM((2, 72, 16, NZ), BF16),
            pltpu.VMEM((60, NY, NZ), F32),
            pltpu.VMEM((72, NY, NZ), F32),
            pltpu.VMEM((60, NY, NZ), F32),
            pltpu.VMEM((48, NY, NZ), F32),
            pltpu.VMEM((36, NY, NZ), F32),
            pltpu.VMEM((2, 24, NY, NZ), F32),
            pltpu.VMEM((2,) + planes, BF16),
            pltpu.VMEM((16,) + planes, BF16),
            pltpu.VMEM((2,) + planes, F32),
            pltpu.VMEM((1024, 256), F32),
            pltpu.VMEM((2, 16, 64), F32),
            pltpu.VMEM((8, 16, 64), F32),
            pltpu.VMEM((4, 16, 64), F32),
            pltpu.SemaphoreType.DMA((10,)),
            pltpu.SemaphoreType.DMA((44,)),
            pltpu.SemaphoreType.DMA((44,)),
        ],
        compiler_params=pltpu.CompilerParams(collective_id=0, has_side_effects=True, vmem_limit_bytes=int(52.5 * 2**20)),
    )(block, potential, stored)
    return filtered, inter.T


def solution(mesh):
    in_specs = (P("orb", "dom", None, None), P("dom", None, None), P("orb", "dom", None, None))
    out_specs = (P("orb", "dom", None, None), P("orb", None))
    return jax.shard_map(body, mesh=mesh, in_specs=in_specs, out_specs=out_specs, check_vma=False)
```

```python
import jax
import jax.numpy as jnp
import ml_dtypes
import numpy as np
from jax import lax
from jax.experimental import pallas as pl
from jax.experimental.pallas import tpu as pltpu
from jax.sharding import PartitionSpec as P

F32, BF16 = jnp.float32, jnp.bfloat16
MESH = pl.DeviceIdType.MESH

coeffs = (
    -5369.0 / 1800.0,
    12.0 / 7.0,
    -15.0 / 56.0,
    10.0 / 189.0,
    -1.0 / 112.0,
    2.0 / 825.0,
    -1.0 / 5544.0,
)
WEIGHTS = tuple(-0.5 * 6.25 * c / 16.0 for c in coeffs)
SHIFT = (-0.5 * 6.25 * 3.0 * coeffs[0] - 36.0) / 16.0
CX, NY, NZ = 12, 32, 128
PAIRS, SLABS = 16, 32


HIGHS = tuple(float(np.float32(w).astype(ml_dtypes.bfloat16)) for w in WEIGHTS)
LOWS = tuple(w - high for w, high in zip(WEIGHTS, HIGHS))


def iotas(shape):
    return lax.broadcasted_iota(jnp.int32, shape, 0), lax.broadcasted_iota(jnp.int32, shape, 1)


def circulant(n, values):
    i, j = iotas((n, n))
    distance = (i - j) & (n - 1)
    matrix = jnp.zeros((n, n), F32)
    for m in range(1, 7):
        matrix = jnp.where((distance == m) | (distance == n - m), values[m], matrix)
    return matrix


def kernel(
    block, potential, stored, filtered, inter,
    cz_ref, cy_ref, blkf, potf, st, blkb, rb, potb, diag, a0, a1, a2, a3, a4, sendp, low, outf, acc, part, ar1, ar2,
    local_sem, send_sem, recv_sem,
):
    dom, orb = lax.axis_index("dom"), lax.axis_index("orb")
    h = lax.rem(dom, 2)
    pair = dom // 2
    up, down = lax.rem(dom + 2, SLABS), lax.rem(dom + SLABS - 2, SLABS)
    partner = dom + 1 - 2 * h
    core = lax.rem(orb, 2)
    sibling = orb + 1 - 2 * core
    across = lax.rem(orb + 2, 4)
    row, column = lax.rem(dom, 8), dom // 8

    def rowpeer(k):
        return column * 8 + lax.rem(row + k, 8)

    def columnpeer(k):
        return lax.rem(column + k, 4) * 8 + row

    barrier = pltpu.get_barrier_semaphore()
    peers = [(rowpeer(k), orb) for k in (1, 7)] + [(up, orb), (down, orb), (dom, sibling), (dom, across), (partner, across)]
    peers += [(rowpeer(k), orb) for k in range(2, 7)] + [(columnpeer(k), orb) for k in range(1, 4)]
    for peer in peers:
        pl.semaphore_signal(barrier, inc=1, device_id=peer, device_id_type=MESH)

    other = 1 - h
    order = (2 * other, 2 * other + 1, 2 * h, 2 * h + 1)
    loads = [pltpu.make_async_copy(block.at[i], blkf.at[i], local_sem.at[n]) for n, i in enumerate(order)]
    loads.insert(2, pltpu.make_async_copy(potential, potf, local_sem.at[4]))
    load_stored = pltpu.make_async_copy(stored, st, local_sem.at[5])
    for load in loads:
        load.start()
    high, rest = circulant(NZ, HIGHS), circulant(NZ, LOWS)
    cz_ref[...] = jnp.concatenate([jnp.concatenate([high, rest], 1)] * 2, 0).astype(BF16)
    high, rest = circulant(NY, HIGHS), circulant(NY, LOWS)
    cy_ref[...] = jnp.concatenate([jnp.concatenate([high, high], 1), jnp.concatenate([rest, rest], 1)], 0).astype(BF16)
    for load in loads:
        load.wait()
    load_stored.start()
    for i in range(4):
        blkb[i] = blkf[i].astype(BF16)
    for r in range(2):
        potb[r, pl.ds(24 + 12 * h, 12)] = potf[:, 16 * r : 16 * r + 16].astype(BF16)

    pl.semaphore_wait(barrier, len(peers))

    def remote(i, src, dst, peer):
        return pltpu.make_async_remote_copy(
            src_ref=src, dst_ref=dst, send_sem=send_sem.at[i], recv_sem=recv_sem.at[i],
            device_id=peer, device_id_type=MESH,
        )

    def swap(o):
        return (remote(o, blkb.at[2 * other + o], rb.at[o, 2 + h], (partner, orb)),)

    def own(o):
        src = blkb.at[2 * h + o]
        return remote(2 + o, src, rb.at[o, h], (up, orb)), remote(4 + o, src, rb.at[o, 4 + h], (down, orb))

    def forward(o):
        src = rb.at[o, 2 + other]
        return remote(6 + o, src, rb.at[o, other], (up, orb)), remote(8 + o, src, rb.at[o, 4 + other], (down, orb))

    group_low = 4 * orb + 2 * h

    def gather(o):
        here = low.at[group_low + o]
        return (
            remote(10 + o, sendp.at[o], here, (partner, orb)),
            remote(12 + o, sendp.at[o], here, (partner, across)),
            remote(14 + o, here, here, (dom, across)),
            remote(16 + o, here, here, (dom, sibling)),
        )

    def relay(o):
        arrived = (4 * orb + 2 * other + o, 4 * across + 2 * other + o, 4 * across + 2 * h + o)
        return tuple(remote(18 + 2 * n + o, low.at[i], low.at[i], (dom, sibling)) for n, i in enumerate(arrived))

    def pot_copy(i, src, dst, length, peer):
        return remote(i, potb.at[core, pl.ds(src, length)], potb.at[core, pl.ds(dst, length)], peer)

    def pot_copies(i, kind):
        src = 24 + 12 * kind
        rest = 6 * (1 - kind)
        return (
            pot_copy(i, src + 6, 12 * kind + 6, 6, (up, orb)),
            pot_copy(i + 1, src, 48 + 12 * kind, 6, (down, orb)),
            pot_copy(i + 2, src + rest, 48 - 36 * kind + rest, 6, (lax.select(kind == 1, up, down), orb)),
        )

    swap_pot = (pot_copy(24, 24 + 12 * h, 24 + 12 * h, 12, (partner, orb)),)
    own_pot, forward_pot = pot_copies(25, h), pot_copies(28, other)
    share_pot = tuple(
        pot_copy(31 + n, at, at, length, (dom, sibling))
        for n, (at, length) in enumerate(((6, 18), (24 + 12 * other, 12), (48, 18)))
    )

    def start(copies):
        for copy in copies:
            copy.start()

    def received(copies):
        for copy in copies:
            copy.wait_recv()

    def sent(copies):
        for copy in copies:
            copy.wait_send()

    start(swap_pot + own_pot + swap(0) + own(0))
    received(swap_pot)
    start(forward_pot + swap(1))
    received(swap(0))
    start(forward(0) + own(1))
    received(swap(1))
    start(forward(1))

    in_low = jnp.where(pair > 0, 1.0, 0.0).astype(F32)
    in_high = jnp.where(pair < PAIRS - 1, 1.0, 0.0).astype(F32)

    received(own_pot + forward_pot)
    start(share_pot)
    received(share_pot)
    for r in range(2):
        diag[:, 16 * r : 16 * r + 16] = potb[r, 6:66].astype(F32) * (1.0 / 16.0) + SHIFT
    diag[pl.ds(18 + 12 * h, 12)] = potf[...] * (1.0 / 16.0) + SHIFT

    def step(src, src_at, prev, prev_at, dst, dst_at, starts, masked=True):
        for e in starts:
            s = e - src_at
            for i in range(0, 12, 2):
                v = src[pl.ds(s + i, 2)].reshape(2 * NY, NZ)
                high = v.astype(BF16)
                rest = (v - high.astype(F32)).astype(BF16)
                along_z = jnp.dot(jnp.concatenate([high, rest], 1), cz_ref[...], preferred_element_type=F32)
                along_z = along_z[:, :NZ] + along_z[:, NZ:]
                parts = [jnp.concatenate([a[NY * k : NY * k + NY] for a in (high, rest)], 0) for k in range(2)]
                along_y = jnp.dot(cy_ref[...], jnp.concatenate(parts, 1), preferred_element_type=F32)
                along_y = along_y[:NY] + along_y[NY:]
                for k in range(2):
                    dst[e + i + k - dst_at] = along_z[NY * k : NY * k + NY] + along_y[:, NZ * k : NZ * k + NZ]
            for y in range(0, NY, 16):
                window = [src[s - 6 + k, y : y + 16].astype(BF16) for k in range(24)]
                for i in range(12):
                    t = None
                    for m in range(6, 2, -1):
                        term = jnp.bfloat16(WEIGHTS[m]) * (window[6 + i + m] + window[6 + i - m])
                        t = term if t is None else t + term
                    at = e + i - dst_at
                    dst[at, y : y + 16] = dst[at, y : y + 16] + t.astype(F32)
            for y in range(0, NY, 8):
                window = [src[s - 6 + k, y : y + 8] for k in range(24)]
                for i in range(12):
                    t = window[6 + i] * diag[e + i - 6, y : y + 8]
                    for m in range(1, 3):
                        t = t + WEIGHTS[m] * (window[6 + i + m] + window[6 + i - m])
                    t = t + dst[e + i - dst_at, y : y + 8]
                    if prev is None:
                        t = t * 0.5
                    else:
                        t = t - prev[e + i - prev_at, y : y + 8]
                    if masked and e + i < 24:
                        t = t * in_low
                    elif masked and e + i >= 48:
                        t = t * in_high
                    dst[e + i - dst_at, y : y + 8] = t

    def out_own(o):
        return pltpu.make_async_copy(a4.at[o, pl.ds(12 * h, 12)], filtered.at[2 * h + o], local_sem.at[6 + o])

    def out_other(o):
        return pltpu.make_async_copy(outf.at[o], filtered.at[2 * other + o], local_sem.at[8 + o])

    def orbital(o, carry):
        received(own(o) + forward(o))
        for slab in (0, 1, 4, 5):
            a0[12 * slab : 12 * slab + 12] = rb[o, slab].astype(F32) * (in_low if slab < 2 else in_high)
        a0[pl.ds(24 + 12 * other, 12)] = rb[o, 2 + other].astype(F32)
        a0[pl.ds(24 + 12 * h, 12)] = blkf[2 * h + o]
        step(a0, 0, None, 0, a1, 6, range(6, 66, 12))
        step(a1, 6, a0, 0, a2, 12, range(12, 60, 12))
        step(a2, 12, a1, 6, a3, 18, range(18, 54, 12))
        step(a3, 18, a2, 12, a4.at[o], 24, (24 + 12 * other,), masked=False)
        sendp[o] = a4[o, pl.ds(12 * other, 12)].astype(BF16)
        start(gather(o)[:2])
        step(a3, 18, a2, 12, a4.at[o], 24, (24 + 12 * h,), masked=False)
        low[group_low + o] = a4[o, pl.ds(12 * h, 12)].astype(BF16)
        start(gather(o)[2:])
        out_own(o).start()
        return carry

    lax.fori_loop(0, 2, orbital, 0)

    for o in range(2):
        for i in (2, 1, 0):
            received(gather(o)[i : i + 1])
            start(relay(o)[i : i + 1])
        outf[o] = low[4 * orb + 2 * other + o].astype(F32)
        out_other(o).start()
    for o in range(2):
        received(gather(o)[3:] + relay(o))

    load_stored.wait()
    total = None
    for p in range(0, 12, 2):
        for y in range(0, NY, 16):
            left = [st[:, p + i, y : y + 16].reshape(1024, NZ) for i in range(2)]
            right = [low[:, p + i, y : y + 16].reshape(256, NZ) for i in range(2)]
            term = lax.dot_general(
                jnp.concatenate(left, 1), jnp.concatenate(right, 1), (((1,), (1,)), ((), ())), preferred_element_type=F32
            )
            total = term if total is None else total + term
    acc[...] = total
    i, j = iotas((16, 256))
    same = i == j % 16
    rows = jnp.sum(jnp.where(same[None], acc[...].reshape(64, 16, 256), 0.0), axis=1)
    first = rows.astype(BF16)
    rest = rows - first.astype(F32)
    second = rest.astype(BF16)
    third = (rest - second.astype(F32)).astype(BF16)
    i, j = iotas((16, 256))
    fold = jnp.where(i == j // 16, 1.0, 0.0).astype(BF16)
    total = jnp.zeros((16, 64), F32)
    for piece in (third, second, first):
        total = total + lax.dot_general(fold, piece, (((1,), (1,)), ((), ())), preferred_element_type=F32)

    sums = []
    for buffer, size, me, peer in ((ar1, 8, row, rowpeer), (ar2, 4, column, columnpeer)):
        part_at = part.at[0 if size == 8 else 1]
        part_at[...] = total
        buffer[me] = total
        at = 33 if size == 8 else 40
        copies = [remote(at + k, part_at, buffer.at[me], (peer(k), orb)) for k in range(1, size)]
        start(copies)
        received(copies)
        total = buffer[0]
        for k in range(1, size):
            total = total + buffer[k]
        sums += copies
    inter[...] = total

    sent(sums)
    sent(swap_pot + own_pot + forward_pot + share_pot)
    for o in range(2):
        sent(swap(o) + own(o) + forward(o) + gather(o) + relay(o))
        out_own(o).wait()
        out_other(o).wait()


def body(block, potential, stored):
    planes = (CX, NY, NZ)
    vmem, anywhere = pl.BlockSpec(memory_space=pltpu.VMEM), pl.BlockSpec(memory_space=pl.ANY)
    filtered, inter = pl.pallas_call(
        kernel,
        out_shape=(jax.ShapeDtypeStruct((4,) + planes, F32), jax.ShapeDtypeStruct((16, 64), F32)),
        in_specs=[anywhere] * 3,
        out_specs=(anywhere, vmem),
        scratch_shapes=[
            pltpu.VMEM((256, 256), BF16),
            pltpu.VMEM((64, 64), BF16),
            pltpu.VMEM((4,) + planes, F32),
            pltpu.VMEM(planes, F32),
            pltpu.VMEM((64,) + planes, BF16),
            pltpu.VMEM((4,) + planes, BF16),
            pltpu.VMEM((2, 6) + planes, BF16),
            pltpu.VMEM((2, 72, 16, NZ), BF16),
            pltpu.VMEM((60, NY, NZ), F32),
            pltpu.VMEM((72, NY, NZ), F32),
            pltpu.VMEM((60, NY, NZ), F32),
            pltpu.VMEM((48, NY, NZ), F32),
            pltpu.VMEM((36, NY, NZ), F32),
            pltpu.VMEM((2, 24, NY, NZ), F32),
            pltpu.VMEM((2,) + planes, BF16),
            pltpu.VMEM((16,) + planes, BF16),
            pltpu.VMEM((2,) + planes, F32),
            pltpu.VMEM((1024, 256), F32),
            pltpu.VMEM((2, 16, 64), F32),
            pltpu.VMEM((8, 16, 64), F32),
            pltpu.VMEM((4, 16, 64), F32),
            pltpu.SemaphoreType.DMA((10,)),
            pltpu.SemaphoreType.DMA((44,)),
            pltpu.SemaphoreType.DMA((44,)),
        ],
        compiler_params=pltpu.CompilerParams(collective_id=0, has_side_effects=True, vmem_limit_bytes=int(52.5 * 2**20)),
    )(block, potential, stored)
    return filtered, inter.T


def solution(mesh):
    in_specs = (P("orb", "dom", None, None), P("dom", None, None), P("orb", "dom", None, None))
    out_specs = (P("orb", "dom", None, None), P("orb", None))
    return jax.shard_map(body, mesh=mesh, in_specs=in_specs, out_specs=out_specs, check_vma=False)
```

```python
import jax
import jax.numpy as jnp
import ml_dtypes
import numpy as np
from jax import lax
from jax.experimental import pallas as pl
from jax.experimental.pallas import tpu as pltpu
from jax.sharding import PartitionSpec as P

F32, BF16 = jnp.float32, jnp.bfloat16
MESH = pl.DeviceIdType.MESH

coeffs = (
    -5369.0 / 1800.0,
    12.0 / 7.0,
    -15.0 / 56.0,
    10.0 / 189.0,
    -1.0 / 112.0,
    2.0 / 825.0,
    -1.0 / 5544.0,
)
WEIGHTS = tuple(-0.5 * 6.25 * c / 16.0 for c in coeffs)
SHIFT = (-0.5 * 6.25 * 3.0 * coeffs[0] - 36.0) / 16.0
CX, NY, NZ = 12, 32, 128
PAIRS, SLABS = 16, 32


HIGHS = tuple(float(np.float32(w).astype(ml_dtypes.bfloat16)) for w in WEIGHTS)
LOWS = tuple(w - high for w, high in zip(WEIGHTS, HIGHS))


def iotas(shape):
    return lax.broadcasted_iota(jnp.int32, shape, 0), lax.broadcasted_iota(jnp.int32, shape, 1)


def circulant(n, values):
    i, j = iotas((n, n))
    distance = (i - j) & (n - 1)
    matrix = jnp.zeros((n, n), F32)
    for m in range(1, 7):
        matrix = jnp.where((distance == m) | (distance == n - m), values[m], matrix)
    return matrix


def kernel(
    block, potential, stored, filtered, inter,
    cz_ref, cy_ref, blkf, potf, st, blkb, rb, potb, diag, a0, a1, a2, a3, a4, sendp, low, outf, acc, part, ar1, ar2,
    local_sem, send_sem, recv_sem,
):
    dom, orb = lax.axis_index("dom"), lax.axis_index("orb")
    h = lax.rem(dom, 2)
    pair = dom // 2
    up, down = lax.rem(dom + 2, SLABS), lax.rem(dom + SLABS - 2, SLABS)
    partner = dom + 1 - 2 * h
    core = lax.rem(orb, 2)
    sibling = orb + 1 - 2 * core
    across = lax.rem(orb + 2, 4)
    row, column = lax.rem(dom, 8), dom // 8

    def rowpeer(k):
        return column * 8 + lax.rem(row + k, 8)

    def columnpeer(k):
        return lax.rem(column + k, 4) * 8 + row

    barrier = pltpu.get_barrier_semaphore()
    peers = [(rowpeer(k), orb) for k in (1, 7)] + [(up, orb), (down, orb), (dom, sibling), (dom, across), (partner, across)]
    peers += [(rowpeer(k), orb) for k in range(2, 7)] + [(columnpeer(k), orb) for k in range(1, 4)]
    for peer in peers:
        pl.semaphore_signal(barrier, inc=1, device_id=peer, device_id_type=MESH)

    other = 1 - h
    order = (2 * other, 2 * other + 1, 2 * h, 2 * h + 1)
    loads = [pltpu.make_async_copy(block.at[i], blkf.at[i], local_sem.at[n]) for n, i in enumerate(order)]
    loads.insert(2, pltpu.make_async_copy(potential, potf, local_sem.at[4]))
    load_stored = pltpu.make_async_copy(stored, st, local_sem.at[5])
    for load in loads:
        load.start()
    high, rest = circulant(NZ, HIGHS), circulant(NZ, LOWS)
    cz_ref[...] = jnp.concatenate([jnp.concatenate([high, rest], 1)] * 2, 0).astype(BF16)
    high, rest = circulant(NY, HIGHS), circulant(NY, LOWS)
    cy_ref[...] = jnp.concatenate([jnp.concatenate([high, high], 1), jnp.concatenate([rest, rest], 1)], 0).astype(BF16)
    for load in loads[:3]:
        load.wait()
    for i in order[:2]:
        blkb[i] = blkf[i].astype(BF16)
    for r in range(2):
        potb[r, pl.ds(24 + 12 * h, 12)] = potf[:, 16 * r : 16 * r + 16].astype(BF16)

    pl.semaphore_wait(barrier, len(peers))

    def remote(i, src, dst, peer):
        return pltpu.make_async_remote_copy(
            src_ref=src, dst_ref=dst, send_sem=send_sem.at[i], recv_sem=recv_sem.at[i],
            device_id=peer, device_id_type=MESH,
        )

    def swap(o):
        return (remote(o, blkb.at[2 * other + o], rb.at[o, 2 + h], (partner, orb)),)

    def own(o):
        src = blkb.at[2 * h + o]
        return remote(2 + o, src, rb.at[o, h], (up, orb)), remote(4 + o, src, rb.at[o, 4 + h], (down, orb))

    def forward(o):
        src = rb.at[o, 2 + other]
        return remote(6 + o, src, rb.at[o, other], (up, orb)), remote(8 + o, src, rb.at[o, 4 + other], (down, orb))

    group_low = 4 * orb + 2 * h

    def gather(o):
        here = low.at[group_low + o]
        return (
            remote(10 + o, sendp.at[o], here, (partner, orb)),
            remote(12 + o, sendp.at[o], here, (partner, across)),
            remote(14 + o, here, here, (dom, across)),
            remote(16 + o, here, here, (dom, sibling)),
        )

    def relay(o):
        arrived = (4 * orb + 2 * other + o, 4 * across + 2 * other + o, 4 * across + 2 * h + o)
        return tuple(remote(18 + 2 * n + o, low.at[i], low.at[i], (dom, sibling)) for n, i in enumerate(arrived))

    def pot_copy(i, src, dst, length, peer):
        return remote(i, potb.at[core, pl.ds(src, length)], potb.at[core, pl.ds(dst, length)], peer)

    def pot_copies(i, kind):
        src = 24 + 12 * kind
        rest = 6 * (1 - kind)
        return (
            pot_copy(i, src + 6, 12 * kind + 6, 6, (up, orb)),
            pot_copy(i + 1, src, 48 + 12 * kind, 6, (down, orb)),
            pot_copy(i + 2, src + rest, 48 - 36 * kind + rest, 6, (lax.select(kind == 1, up, down), orb)),
        )

    swap_pot = (pot_copy(24, 24 + 12 * h, 24 + 12 * h, 12, (partner, orb)),)
    own_pot, forward_pot = pot_copies(25, h), pot_copies(28, other)
    share_pot = tuple(
        pot_copy(31 + n, at, at, length, (dom, sibling))
        for n, (at, length) in enumerate(((6, 18), (24 + 12 * other, 12), (48, 18)))
    )

    def start(copies):
        for copy in copies:
            copy.start()

    def received(copies):
        for copy in copies:
            copy.wait_recv()

    def sent(copies):
        for copy in copies:
            copy.wait_send()

    start(swap_pot + swap(0) + own_pot)
    for load in loads[3:]:
        load.wait()
    for i in order[2:]:
        blkb[i] = blkf[i].astype(BF16)
    start(own(0))
    load_stored.start()
    received(swap_pot)
    start(forward_pot + swap(1))
    received(swap(0))
    start(forward(0) + own(1))
    received(swap(1))
    start(forward(1))

    in_low = jnp.where(pair > 0, 1.0, 0.0).astype(F32)
    in_high = jnp.where(pair < PAIRS - 1, 1.0, 0.0).astype(F32)

    received(own_pot + forward_pot)
    start(share_pot)
    received(share_pot)
    for r in range(2):
        diag[:, 16 * r : 16 * r + 16] = potb[r, 6:66].astype(F32) * (1.0 / 16.0) + SHIFT
    diag[pl.ds(18 + 12 * h, 12)] = potf[...] * (1.0 / 16.0) + SHIFT

    def step(src, src_at, prev, prev_at, dst, dst_at, starts, masked=True):
        for e in starts:
            s = e - src_at
            for i in range(0, 12, 2):
                v = src[pl.ds(s + i, 2)].reshape(2 * NY, NZ)
                high = v.astype(BF16)
                rest = (v - high.astype(F32)).astype(BF16)
                along_z = jnp.dot(jnp.concatenate([high, rest], 1), cz_ref[...], preferred_element_type=F32)
                along_z = along_z[:, :NZ] + along_z[:, NZ:]
                parts = [jnp.concatenate([a[NY * k : NY * k + NY] for a in (high, rest)], 0) for k in range(2)]
                along_y = jnp.dot(cy_ref[...], jnp.concatenate(parts, 1), preferred_element_type=F32)
                along_y = along_y[:NY] + along_y[NY:]
                for k in range(2):
                    dst[e + i + k - dst_at] = along_z[NY * k : NY * k + NY] + along_y[:, NZ * k : NZ * k + NZ]
            for y in range(0, NY, 16):
                window = [src[s - 6 + k, y : y + 16].astype(BF16) for k in range(24)]
                for i in range(12):
                    t = None
                    for m in range(6, 2, -1):
                        term = jnp.bfloat16(WEIGHTS[m]) * (window[6 + i + m] + window[6 + i - m])
                        t = term if t is None else t + term
                    at = e + i - dst_at
                    dst[at, y : y + 16] = dst[at, y : y + 16] + t.astype(F32)
            for y in range(0, NY, 8):
                window = [src[s - 6 + k, y : y + 8] for k in range(24)]
                for i in range(12):
                    t = window[6 + i] * diag[e + i - 6, y : y + 8]
                    for m in range(1, 3):
                        t = t + WEIGHTS[m] * (window[6 + i + m] + window[6 + i - m])
                    t = t + dst[e + i - dst_at, y : y + 8]
                    if prev is None:
                        t = t * 0.5
                    else:
                        t = t - prev[e + i - prev_at, y : y + 8]
                    if masked and e + i < 24:
                        t = t * in_low
                    elif masked and e + i >= 48:
                        t = t * in_high
                    dst[e + i - dst_at, y : y + 8] = t

    def out_own(o):
        return pltpu.make_async_copy(a4.at[o, pl.ds(12 * h, 12)], filtered.at[2 * h + o], local_sem.at[6 + o])

    def out_other(o):
        return pltpu.make_async_copy(outf.at[o], filtered.at[2 * other + o], local_sem.at[8 + o])

    def orbital(o, carry):
        received(own(o) + forward(o))
        for slab in (0, 1, 4, 5):
            a0[12 * slab : 12 * slab + 12] = rb[o, slab].astype(F32) * (in_low if slab < 2 else in_high)
        a0[pl.ds(24 + 12 * other, 12)] = rb[o, 2 + other].astype(F32)
        a0[pl.ds(24 + 12 * h, 12)] = blkf[2 * h + o]
        step(a0, 0, None, 0, a1, 6, range(6, 66, 12))
        step(a1, 6, a0, 0, a2, 12, range(12, 60, 12))
        step(a2, 12, a1, 6, a3, 18, range(18, 54, 12))
        step(a3, 18, a2, 12, a4.at[o], 24, (24 + 12 * other,), masked=False)
        sendp[o] = a4[o, pl.ds(12 * other, 12)].astype(BF16)
        start(gather(o)[:2])
        step(a3, 18, a2, 12, a4.at[o], 24, (24 + 12 * h,), masked=False)
        low[group_low + o] = a4[o, pl.ds(12 * h, 12)].astype(BF16)
        start(gather(o)[2:])
        out_own(o).start()
        return carry

    lax.fori_loop(0, 2, orbital, 0)

    for o in range(2):
        for i in (2, 1, 0):
            received(gather(o)[i : i + 1])
            start(relay(o)[i : i + 1])
        outf[o] = low[4 * orb + 2 * other + o].astype(F32)
        out_other(o).start()
    for o in range(2):
        received(gather(o)[3:] + relay(o))

    load_stored.wait()
    total = None
    for p in range(0, 12, 2):
        for y in range(0, NY, 16):
            left = [st[:, p + i, y : y + 16].reshape(1024, NZ) for i in range(2)]
            right = [low[:, p + i, y : y + 16].reshape(256, NZ) for i in range(2)]
            term = lax.dot_general(
                jnp.concatenate(left, 1), jnp.concatenate(right, 1), (((1,), (1,)), ((), ())), preferred_element_type=F32
            )
            total = term if total is None else total + term
    acc[...] = total
    i, j = iotas((16, 256))
    same = i == j % 16
    rows = jnp.sum(jnp.where(same[None], acc[...].reshape(64, 16, 256), 0.0), axis=1)
    first = rows.astype(BF16)
    rest = rows - first.astype(F32)
    second = rest.astype(BF16)
    third = (rest - second.astype(F32)).astype(BF16)
    i, j = iotas((16, 256))
    fold = jnp.where(i == j // 16, 1.0, 0.0).astype(BF16)
    total = jnp.zeros((16, 64), F32)
    for piece in (third, second, first):
        total = total + lax.dot_general(fold, piece, (((1,), (1,)), ((), ())), preferred_element_type=F32)

    sums = []
    for buffer, size, me, peer in ((ar1, 8, row, rowpeer), (ar2, 4, column, columnpeer)):
        part_at = part.at[0 if size == 8 else 1]
        part_at[...] = total
        buffer[me] = total
        at = 33 if size == 8 else 40
        copies = [remote(at + k, part_at, buffer.at[me], (peer(k), orb)) for k in range(1, size)]
        start(copies)
        received(copies)
        total = buffer[0]
        for k in range(1, size):
            total = total + buffer[k]
        sums += copies
    inter[...] = total

    sent(sums)
    sent(swap_pot + own_pot + forward_pot + share_pot)
    for o in range(2):
        sent(swap(o) + own(o) + forward(o) + gather(o) + relay(o))
        out_own(o).wait()
        out_other(o).wait()


def body(block, potential, stored):
    planes = (CX, NY, NZ)
    vmem, anywhere = pl.BlockSpec(memory_space=pltpu.VMEM), pl.BlockSpec(memory_space=pl.ANY)
    filtered, inter = pl.pallas_call(
        kernel,
        out_shape=(jax.ShapeDtypeStruct((4,) + planes, F32), jax.ShapeDtypeStruct((16, 64), F32)),
        in_specs=[anywhere] * 3,
        out_specs=(anywhere, vmem),
        scratch_shapes=[
            pltpu.VMEM((256, 256), BF16),
            pltpu.VMEM((64, 64), BF16),
            pltpu.VMEM((4,) + planes, F32),
            pltpu.VMEM(planes, F32),
            pltpu.VMEM((64,) + planes, BF16),
            pltpu.VMEM((4,) + planes, BF16),
            pltpu.VMEM((2, 6) + planes, BF16),
            pltpu.VMEM((2, 72, 16, NZ), BF16),
            pltpu.VMEM((60, NY, NZ), F32),
            pltpu.VMEM((72, NY, NZ), F32),
            pltpu.VMEM((60, NY, NZ), F32),
            pltpu.VMEM((48, NY, NZ), F32),
            pltpu.VMEM((36, NY, NZ), F32),
            pltpu.VMEM((2, 24, NY, NZ), F32),
            pltpu.VMEM((2,) + planes, BF16),
            pltpu.VMEM((16,) + planes, BF16),
            pltpu.VMEM((2,) + planes, F32),
            pltpu.VMEM((1024, 256), F32),
            pltpu.VMEM((2, 16, 64), F32),
            pltpu.VMEM((8, 16, 64), F32),
            pltpu.VMEM((4, 16, 64), F32),
            pltpu.SemaphoreType.DMA((10,)),
            pltpu.SemaphoreType.DMA((44,)),
            pltpu.SemaphoreType.DMA((44,)),
        ],
        compiler_params=pltpu.CompilerParams(collective_id=0, has_side_effects=True, vmem_limit_bytes=int(52.5 * 2**20)),
    )(block, potential, stored)
    return filtered, inter.T


def solution(mesh):
    in_specs = (P("orb", "dom", None, None), P("dom", None, None), P("orb", "dom", None, None))
    out_specs = (P("orb", "dom", None, None), P("orb", None))
    return jax.shard_map(body, mesh=mesh, in_specs=in_specs, out_specs=out_specs, check_vma=False)
```
